1024 devices in a mesh: node: 8 (over y_lo, core), dp: 128 (over z, x, y_hi).
Axes of the slice: x: 8, y: 8 (y_hi: 2, y_lo: 4; y = y_hi * 4 + y_lo), z: 8, core: 2. Of those that a mesh axis runs over, the one named last changes fastest.
Arguments:
- activations: bfloat16 [131072, 4096], P(('node', 'dp')), may hold values from -24 to 24
- key_grads: bfloat16 [131072, 512], P(('node', 'dp')), may hold values from -6 to 6
- w_blocks: bfloat16 [4096, 512], P('node'), may hold values from -0.25 to 0.25
- w_scales: bfloat16 [32, 1], P('node'), may hold values from 0.5 to 2
- w_outliers: bfloat16 [64, 512], P('node'), may hold values from -1 to 1
- outlier_rows: int32 [32, 2], replicated, may hold values from 0 to 127, as said below
Outputs:
- input_grads: bfloat16 [131072, 4096], P(('node', 'dp'))
- weight_grad: float32 [4096, 512], P(('node', 'dp'))
The draws below stay inside these ranges and needn't reach their ends.
Inputs may be any that keep to these rules, and one draw needn't show every extreme that they name: `outlier_rows`: the 2 entries of one block are distinct.
All inputs are finite; a program needn't handle non-finite values.
Results may differ from the reference program's by a relative error of at most 0.015.
Values may be sent and summed in bfloat16 or wider, within the bound.
A program may use at most 32 MiB of HBM per device.

```python
import math
import jax
import jax.numpy as jnp
from jax import lax

D = 4096
KW = 512
BLOCK = 128
OUTL = 2
TOK_DEV = 128
NB = 32
TOKENS = 131072
N_NODE = 8
N_DP = 128


def draw_outlier_rows(key, part):
    key = jax.random.fold_in(key, 11)
    perm_key, block_key = jax.random.split(key, 2)
    block_keys = jax.random.split(perm_key, NB)
    orders = jax.vmap(lambda item_key: jax.random.permutation(item_key, BLOCK))(block_keys)[:, :OUTL]
    chosen = jax.random.randint(block_key, (), 0, NB)
    on_chosen = lax.broadcasted_iota(jnp.int32, (NB, 1), 0) == chosen
    swapped = jnp.where(orders == BLOCK - 1, orders[:, :1], orders)
    fixed = jnp.where(on_chosen, swapped, orders)
    first_col = jnp.where(on_chosen[:, 0], BLOCK - 1, fixed[:, 0])
    return fixed.at[:, 0].set(first_col).astype(jnp.int32)


def with_spikes(values, key, source, target, parts, factor):
    owner, partner = [(jnp.arange(values.shape[axis_at]) // (values.shape[axis_at] // parts)).reshape([-1 if axis == axis_at else 1 for axis in range(values.ndim)]) for axis_at in (source, target)]
    chosen = jax.random.permutation(key, parts)[partner]
    strong = (owner == chosen) | (owner == (partner + parts // 2) % parts)
    return jnp.where(strong, factor * values, values)


def steps_of(key, dims, cuts, low, top_value):
    def one(dim, parts):
        steps = jax.random.uniform(jax.random.fold_in(jax.random.fold_in(key, 6), dim), (parts,), jnp.float32, low / len(cuts), top_value / len(cuts))
        return jnp.repeat(jnp.exp(steps), dims[dim] // parts).reshape((-1,) + (1,) * (len(dims) - dim - 1))

    gain = one(*cuts[0])
    for cut in cuts[1:]:
        gain = gain * one(*cut)
    return gain


def normal_values(stream_key, extent, deviation, reach, cuts=(), kind=jnp.bfloat16):
    array = jax.random.normal(stream_key, extent, jnp.float32) * deviation
    if len(cuts) > 0:
        array = steps_of(stream_key, extent, cuts, -0.22, 0.18) * array
    return jnp.clip(array, min=-reach, max=reach).astype(kind)


def bell_draw_with(stream_key, extent, scale, limit, shards, heavy, dtype=jnp.bfloat16):
    array = scale * jax.random.normal(stream_key, extent, jnp.float32)
    if shards:
        array = array * steps_of(stream_key, extent, shards, -0.22, 0.18)
    return jnp.clip(with_spikes(array, jax.random.fold_in(stream_key, 3), *heavy), -limit, limit).astype(dtype)


def setup_inputs(seed: int = 0) -> dict:
    splits = jax.random.split(jax.random.key(seed), 7)
    return {
        "activations": bell_draw_with(splits[0], (TOKENS, D), 1.0, 24.0, ((0, 1024),), (0, 1, 1024, 6.0)),
        "key_grads": normal_values(splits[1], (TOKENS, KW), 1.0, 6.0, ((0, 1024),)),
        "w_blocks": normal_values(splits[2], (D, KW), KW ** -0.5, 0.25, ((0, 8),)),
        "w_scales": jnp.clip(jnp.exp(math.log(2.0) - 1.3862944 * jax.random.uniform(splits[3], (NB, 1), jnp.float32) ** steps_of(splits[3], (NB, 1), ((0, 8),), -0.2, 0.2)), 0.5, 2.0).astype(jnp.bfloat16),
        "w_outliers": normal_values(splits[4], (NB * OUTL, KW), (KW // 16) ** -0.5, 1.0, ((0, 8),)),
        "outlier_rows": draw_outlier_rows(jax.random.fold_in(splits[6], 71), 0),
    }


def dequantize(quantized, scales, outlier_vals, row_index):
    blocks_here = row_index.shape[0]
    width = quantized.shape[1]
    values = quantized.reshape(blocks_here, BLOCK, width).astype(jnp.float32) * scales.reshape(blocks_here, 1, 1).astype(jnp.float32)
    extra = outlier_vals.reshape(blocks_here, OUTL, width).astype(jnp.float32)
    positions = lax.broadcasted_iota(jnp.int32, (blocks_here, BLOCK), 1)
    for column in range(OUTL):
        chosen_rows = positions == row_index[:, column:column + 1]
        values = jnp.where(chosen_rows[:, :, None], extra[:, column:column + 1, :], values)
    return values.reshape(blocks_here * BLOCK, width).astype(jnp.bfloat16)

def outlier_mask(row_index):
    blocks_here = row_index.shape[0]
    positions = lax.broadcasted_iota(jnp.int32, (blocks_here, BLOCK), 1)
    marked = positions < 0
    for column in range(OUTL):
        marked = jnp.logical_or(marked, positions == row_index[:, column:column + 1])
    return marked

def reference(activations, key_grads, w_blocks, w_scales, w_outliers, outlier_rows):
    weight = dequantize(w_blocks, w_scales, w_outliers, outlier_rows)
    input_grads = lax.dot_general(key_grads, weight, (((1,), (1,)), ((), ())), preferred_element_type=jnp.float32).astype(jnp.bfloat16)
    devices_all = N_NODE * N_DP
    loss_scale = 1.0 / jnp.sqrt(jnp.float32(TOKENS))
    marked = outlier_mask(outlier_rows)
    act_dev = activations.reshape(devices_all, TOK_DEV, D)
    key_dev = key_grads.reshape(devices_all, TOK_DEV, KW)
    pick = jnp.broadcast_to(outlier_rows[:, :, None], (NB, OUTL, KW))

    def add_device(carry, pair):
        bulk_total, outlier_total = carry
        partial_value = lax.dot_general(pair[0], pair[1], (((0,), (0,)), ((), ())), preferred_element_type=jnp.float32) * loss_scale
        blocks3 = partial_value.reshape(NB, BLOCK, KW)
        rounded = jnp.where(marked[:, :, None], 0.0, blocks3).astype(jnp.bfloat16)
        rounded = lax.optimization_barrier(rounded)
        bulk_total = bulk_total + rounded.astype(jnp.float32)
        outlier_total = outlier_total + jnp.take_along_axis(blocks3, pick, axis=1)
        return ((bulk_total, outlier_total), None)
    start = (jnp.zeros((NB, BLOCK, KW), jnp.float32), jnp.zeros((NB, OUTL, KW), jnp.float32))
    (bulk_total, outlier_total), _ = lax.scan(add_device, start, (act_dev, key_dev))
    positions = lax.broadcasted_iota(jnp.int32, (NB, BLOCK), 1)
    merged = bulk_total
    for column in range(OUTL):
        chosen_rows = positions == outlier_rows[:, column:column + 1]
        merged = jnp.where(chosen_rows[:, :, None], outlier_total[:, column:column + 1, :], merged)
    return (input_grads, merged.reshape(D, KW))
```

```python
import jax
import jax.numpy as jnp
from jax import lax
from jax.experimental import pallas as pl
from jax.experimental.pallas import tpu as pltpu
from jax.sharding import PartitionSpec as P

D = 4096
KW = 512
BLOCK = 128
TOK = 128
TOKENS = 131072
RING = 8
YLO = 4
MESH = pl.DeviceIdType.MESH


def kernel(
    act, key, wq, scales, wout, rows,
    ig, wg,
    a_all, k_all, w_raw, w_all, part0, part1, ring_in, s2_in, s3_out, s3_in, ig_own, ig_sib,
    loc_sem, ex_send, ex_recv, w_send, w_recv, ring_send, ring_recv,
    s2_send, s2_recv, s3_send, s3_recv, ig_loc, ig_send, ig_recv,
):
    node, dp = lax.axis_index("node"), lax.axis_index("dp")
    core, ylo = node % 2, node // 2
    z, x, yhi = dp // 16, (dp // 2) % 8, dp % 2
    y = yhi * 4 + ylo
    part = (part0, part1)
    place = (x, z)

    def at(px, py, pz, pc):
        return ((py % 4) * 2 + pc, pz * 16 + px * 2 + py // 4)

    def on_x(step):
        return at((x + step) % RING, y, z, core)

    def on_y(step):
        return at(x, (y + step) % RING, z, core)

    def on_z(step):
        return at(x, y, (z + step) % RING, core)

    sibling = at(x, y, z, 1 - core)
    first_axis = (on_x, on_z)
    second_axis = (on_z, on_x)

    def columns(block, whose):
        return pl.ds(pl.multiple_of((2 * block + whose) * 512, 512), 512)

    def remote(src, dst, send, recv, device):
        return pltpu.make_async_remote_copy(
            src_ref=src, dst_ref=dst, send_sem=send, recv_sem=recv,
            device_id=device, device_id_type=MESH,
        )

    local_w = pltpu.make_async_copy(wq, w_raw, loc_sem.at[0])
    local_k = pltpu.make_async_copy(key, k_all.at[pl.ds(0, TOK)], loc_sem.at[1])
    local_a = [
        pltpu.make_async_copy(
            act.at[:, columns(b, core)],
            a_all.at[pl.ds(0, TOK), pl.ds(b * 512, 512)],
            loc_sem.at[2 + b],
        )
        for b in range(YLO)
    ]
    local_w.start()
    local_k.start()
    for copy in local_a:
        copy.start()

    barrier = pltpu.get_barrier_semaphore()
    pl.semaphore_signal(barrier, inc=1, device_id=sibling, device_id_type=MESH)
    for along in (on_x, on_y, on_z):
        for step in range(1, RING):
            pl.semaphore_signal(barrier, inc=1, device_id=along(step), device_id_type=MESH)

    local_w.wait()
    scale = scales[...].astype(jnp.float32)
    extra = wout[...].astype(jnp.float32)
    spot = lax.broadcasted_iota(jnp.int32, (BLOCK, KW), 0)
    for b in range(4):
        values = w_raw[pl.ds(b * BLOCK, BLOCK), :].astype(jnp.float32) * scale[:, b : b + 1]
        for j in range(2):
            row = rows[j, node * 4 + b]
            values = jnp.where(spot == row, extra[2 * b + j : 2 * b + j + 1, :], values)
        w_all[0, pl.ds(b * BLOCK, BLOCK), :] = values.astype(jnp.bfloat16)

    pl.semaphore_wait(barrier, 1 + 3 * (RING - 1))

    exchange = [remote(key, k_all.at[pl.ds(TOK, TOK)], ex_send.at[4], ex_recv.at[4], sibling)]
    for b in range(YLO):
        exchange.append(
            remote(
                act.at[:, columns(b, 1 - core)],
                a_all.at[pl.ds(TOK, TOK), pl.ds(b * 512, 512)],
                ex_send.at[b], ex_recv.at[b], sibling,
            )
        )
    for copy in exchange:
        copy.start()

    def half(slot, index):
        return w_all.at[slot, pl.ds(index * 256, 256)]

    weight = {}
    for direction, step in ((0, 1), (1, -1)):
        for order in range(2):
            index = order if direction == 0 else 1 - order
            copy = remote(
                half(0, index), half(1 + direction, index),
                w_send.at[direction, order], w_recv.at[direction, order], on_y(step),
            )
            copy.start()
            weight[direction, order] = copy

    def relay_weight():
        for direction, step in ((0, 1), (1, -1)):
            weight[direction, 0].wait_recv()
            copy = remote(
                half(1 + direction, direction), half(3, direction),
                w_send.at[direction, 2], w_recv.at[direction, 2], on_y(step),
            )
            copy.start()
            weight[direction, 2] = copy

    def piece(p, chunk, h):
        return part[p].at[chunk, pl.ds(2 * h, 2)]

    ring = {}

    def send_ring(p, direction, h, hop):
        sign = 1 if direction == 0 else -1
        chunk = (place[p] + sign * (4 - hop)) % RING
        if hop > (0 if h == direction else 1):
            ring[p, direction, h, hop - 1].wait_recv()
            total = part[p][chunk, pl.ds(2 * h, 2)].astype(jnp.float32) + ring_in[
                p, direction, h, hop - 1
            ].astype(jnp.float32)
            part[p][chunk, pl.ds(2 * h, 2)] = total.astype(jnp.bfloat16)
        copy = remote(
            piece(p, chunk, h), ring_in.at[p, direction, h, hop],
            ring_send.at[p, direction, h, hop], ring_recv.at[p, direction, h, hop],
            first_axis[p](sign),
        )
        copy.start()
        ring[p, direction, h, hop] = copy

    def partial(b):
        local_a[b].wait()
        exchange[1 + b].wait_recv()
        product = lax.dot_general(
            a_all[:, pl.ds(b * 512, 512)], k_all[...], (((0,), (0,)), ((), ())),
            preferred_element_type=jnp.float32,
        )
        for p in range(2):
            tiles = [
                product[:, (2 * p + c) * 128 : (2 * p + c + 1) * 128].reshape(8, 8, 8, 128)
                for c in range(2)
            ]
            both = jnp.concatenate(tiles, axis=2).astype(jnp.bfloat16)
            for i in range(8):
                part[p][i, b] = both[:, i] if p == 0 else both[i]

    local_k.wait()
    exchange[0].wait_recv()
    for h in range(2):
        partial(2 * h)
        partial(2 * h + 1)
        for p in range(2):
            send_ring(p, h, h, 0)
        for p in range(2):
            send_ring(p, 1 - h, h, 1)

    grads = {}

    def input_grads(slot, away):
        out = lax.dot_general(
            k_all[...], w_all[slot], (((1,), (1,)), ((), ())), preferred_element_type=jnp.float32
        ).astype(jnp.bfloat16)
        ig_own[slot] = out[:TOK]
        ig_sib[slot] = out[TOK:]
        where = columns((ylo + away) % YLO, core)
        local = pltpu.make_async_copy(ig_own.at[slot], ig.at[:, where], ig_loc.at[slot])
        local.start()
        copy = remote(
            ig_sib.at[slot], ig.at[:, where], ig_send.at[slot], ig_recv.at[slot], sibling
        )
        copy.start()
        grads[slot] = (local, copy)

    input_grads(0, 0)
    for p in range(2):
        for direction in range(2):
            send_ring(p, direction, direction, 1)
    for p in range(2):
        for direction in range(2):
            send_ring(p, direction, 1 - direction, 2)
    relay_weight()
    for p in range(2):
        for direction in range(2):
            send_ring(p, direction, direction, 2)
    for p in range(2):
        for direction in range(2):
            send_ring(p, direction, 1 - direction, 3)
    for p in range(2):
        for direction in range(2):
            send_ring(p, direction, direction, 3)
    for direction, away in ((0, -1), (1, 1)):
        weight[direction, 1].wait_recv()
        input_grads(1 + direction, away)

    other = (z, x)
    second = {}
    for p in range(2):
        for h in range(2):
            total = part[p][place[p], pl.ds(2 * h, 2)].astype(jnp.float32)
            for direction in range(2):
                ring[p, direction, h, 3].wait_recv()
                total = total + ring_in[p, direction, h, 3].astype(jnp.float32)
            part[p][place[p], pl.ds(2 * h, 2)] = total.astype(jnp.bfloat16)
        for step in (4, 3, 5, 2, 6, 1, 7):
            copy = remote(
                part[p].at[place[p], :, (other[p] + step) % RING], s2_in.at[p, step],
                s2_send.at[p, step], s2_recv.at[p, step], second_axis[p](step),
            )
            copy.start()
            second[p, step] = copy

    for direction in range(2):
        weight[direction, 2].wait_recv()
    input_grads(3, 2)

    for p in range(2):
        total = part[p][place[p], :, other[p]].astype(jnp.float32)
        for step in (1, 7, 2, 6, 3, 5, 4):
            second[p, step].wait_recv()
            total = total + s2_in[p, step].astype(jnp.float32)
        s3_out[:, p] = total.astype(jnp.bfloat16)
    third = {}
    for step in (4, 3, 5, 2, 6, 1, 7):
        copy = remote(
            s3_out.at[(ylo + step) % YLO], s3_in.at[step], s3_send.at[step], s3_recv.at[step],
            on_y(step),
        )
        copy.start()
        third[step] = copy
    total = s3_out[ylo].astype(jnp.float32)
    for step in (1, 7, 2, 6, 3, 5, 4):
        third[step].wait_recv()
        total = total + s3_in[step].astype(jnp.float32)
    total = total * (1.0 / TOKENS ** 0.5)
    for p in range(2):
        for c in range(2):
            low, high = total[p, 8 * c : 8 * c + 4], total[p, 8 * c + 4 : 8 * c + 8]
            wg[:, (2 * p + c) * 128 : (2 * p + c + 1) * 128] = jnp.where(yhi == 0, low, high)

    for local, copy in grads.values():
        local.wait()
        copy.wait()
    for copy in exchange:
        copy.wait_send()
    for group in (weight, ring, second, third):
        for copy in group.values():
            copy.wait_send()


def on_device(activations, key_grads, w_blocks, w_scales, w_outliers, outlier_rows):
    bf16, dma = jnp.bfloat16, pltpu.SemaphoreType.DMA
    hbm, vmem = pl.BlockSpec(memory_space=pl.ANY), pl.BlockSpec(memory_space=pltpu.VMEM)
    return pl.pallas_call(
        kernel,
        out_shape=(
            jax.ShapeDtypeStruct((TOK, D), bf16),
            jax.ShapeDtypeStruct((4, KW), jnp.float32),
        ),
        in_specs=[hbm, hbm, hbm, vmem, vmem, pl.BlockSpec(memory_space=pltpu.SMEM)],
        out_specs=(hbm, vmem),
        scratch_shapes=[
            pltpu.VMEM((2 * TOK, D // 2), bf16),
            pltpu.VMEM((2 * TOK, KW), bf16),
            pltpu.VMEM((512, KW), bf16),
            pltpu.VMEM((4, 512, KW), bf16),
            pltpu.VMEM((8, YLO, 8, 16, 128), bf16),
            pltpu.VMEM((8, YLO, 8, 16, 128), bf16),
            pltpu.VMEM((2, 2, 2, 4, 2, 8, 16, 128), bf16),
            pltpu.VMEM((2, 8, YLO, 16, 128), bf16),
            pltpu.VMEM((YLO, 2, 16, 128), bf16),
            pltpu.VMEM((8, 2, 16, 128), bf16),
            pltpu.VMEM((4, TOK, 512), bf16),
            pltpu.VMEM((4, TOK, 512), bf16),
            dma((6,)), dma((5,)), dma((5,)), dma((2, 3)), dma((2, 3)),
            dma((2, 2, 2, 4)), dma((2, 2, 2, 4)),
            dma((2, 8)), dma((2, 8)), dma((8,)), dma((8,)), dma((4,)), dma((4,)), dma((4,)),
        ],
        compiler_params=pltpu.CompilerParams(
            collective_id=0, has_side_effects=True, vmem_limit_bytes=40 * 1024 * 1024
        ),
        cost_estimate=pl.CostEstimate(
            flops=4 * TOK * D * KW, bytes_accessed=4 * 1024 * 1024, transcendentals=0
        ),
    )(
        activations, key_grads, w_blocks, w_scales.reshape(1, -1), w_outliers, outlier_rows.T
    )


def solution(mesh):
    both = P(("node", "dp"), None)
    return jax.shard_map(
        on_device,
        mesh=mesh,
        in_specs=(both, both, P("node", None), P("node", None), P("node", None), P()),
        out_specs=(both, both),
        check_vma=False,
    )
```

```python
import jax
import jax.numpy as jnp
from jax import lax
from jax.experimental import pallas as pl
from jax.experimental.pallas import tpu as pltpu
from jax.sharding import PartitionSpec as P

D = 4096
KW = 512
BLOCK = 128
TOK = 128
TOKENS = 131072
RING = 8
YLO = 4
VMEM_BYTES = 56 * 1024 * 1024
MESH = pl.DeviceIdType.MESH


def kernel(
    act, key, wq, scales_in, wout_in, rows_in,
    ig, wg,
    scales, wout, rows, a_all, k_all, w_raw, w_all, part0, part1, ring_in, s2_in, s3_out, s3_in, ig_own, ig_sib,
    loc_sem, ex_send, ex_recv, w_send, w_recv, ring_send, ring_recv,
    s2_send, s2_recv, s3_send, s3_recv, ig_loc, ig_send, ig_recv,
):
    node, dp = lax.axis_index("node"), lax.axis_index("dp")
    core, ylo = node % 2, node // 2
    z, x, yhi = dp // 16, (dp // 2) % 8, dp % 2
    y = yhi * 4 + ylo
    part = (part0, part1)
    place = (x, z)
    other = (z, x)

    def at(px, py, pz, pc):
        return ((py % 4) * 2 + pc, pz * 16 + px * 2 + py // 4)

    def on_x(step):
        return at((x + step) % RING, y, z, core)

    def on_y(step):
        return at(x, (y + step) % RING, z, core)

    def on_z(step):
        return at(x, y, (z + step) % RING, core)

    sibling = at(x, y, z, 1 - core)
    first_axis = (on_x, on_z)
    second_axis = (on_z, on_x)

    def columns(block, whose):
        return pl.ds(pl.multiple_of((2 * block + whose) * 512, 512), 512)

    def remote(src, dst, send, recv, device):
        return pltpu.make_async_remote_copy(
            src_ref=src, dst_ref=dst, send_sem=send, recv_sem=recv,
            device_id=device, device_id_type=MESH,
        )

    barrier = pltpu.get_barrier_semaphore()
    for step in (4, 3, 5, 2, 6, 1, 7):
        for along in (on_y, on_x, on_z):
            pl.semaphore_signal(barrier, inc=1, device_id=along(step), device_id_type=MESH)
    pl.semaphore_signal(barrier, inc=1, device_id=sibling, device_id_type=MESH)

    local_w = pltpu.make_async_copy(wq, w_raw, loc_sem.at[0])
    local_k = pltpu.make_async_copy(key, k_all.at[pl.ds(0, TOK)], loc_sem.at[1])
    local_a = [
        pltpu.make_async_copy(
            act.at[:, columns(b, core)],
            a_all.at[pl.ds(0, TOK), pl.ds(b * 512, 512)],
            loc_sem.at[2 + b],
        )
        for b in range(YLO)
    ]
    small = [
        pltpu.make_async_copy(src, dst, loc_sem.at[6 + i])
        for i, (src, dst) in enumerate(((scales_in, scales), (wout_in, wout), (rows_in, rows)))
    ]
    for copy in (*small, local_w, local_k, *local_a):
        copy.start()

    pl.semaphore_wait(barrier, 1 + 3 * (RING - 1))

    exchange = [remote(key, k_all.at[pl.ds(TOK, TOK)], ex_send.at[4], ex_recv.at[4], sibling)]
    for b in range(YLO):
        exchange.append(
            remote(
                act.at[:, columns(b, 1 - core)],
                a_all.at[pl.ds(TOK, TOK), pl.ds(b * 512, 512)],
                ex_send.at[b], ex_recv.at[b], sibling,
            )
        )
    for copy in exchange:
        copy.start()

    for copy in (*small, local_w):
        copy.wait()
    scale = scales[...].astype(jnp.float32)
    extra = wout[...].astype(jnp.float32)
    spot = lax.broadcasted_iota(jnp.int32, (BLOCK, KW), 0)
    for b in range(4):
        values = w_raw[pl.ds(b * BLOCK, BLOCK), :].astype(jnp.float32) * scale[:, b : b + 1]
        for j in range(2):
            row = rows[j, node * 4 + b]
            values = jnp.where(spot == row, extra[2 * b + j : 2 * b + j + 1, :], values)
        w_all[0, pl.ds(b * BLOCK, BLOCK), :] = values.astype(jnp.bfloat16)

    def half(slot, index):
        return w_all.at[slot, pl.ds(index * 256, 256)]

    weight = {}
    for direction, step in ((0, 1), (1, -1)):
        for order in range(2):
            index = order if direction == 0 else 1 - order
            copy = remote(
                half(0, index), half(1 + direction, index),
                w_send.at[direction, order], w_recv.at[direction, order], on_y(step),
            )
            copy.start()
            weight[direction, order] = copy

    def relay_weight():
        for direction, step in ((0, 1), (1, -1)):
            weight[direction, 0].wait_recv()
            copy = remote(
                half(1 + direction, direction), half(3, direction),
                w_send.at[direction, 2], w_recv.at[direction, 2], on_y(step),
            )
            copy.start()
            weight[direction, 2] = copy

    order = (0, 1, 3, 2)
    far_end = ((0, 3), (1, 2))

    def piece(p, chunk, s):
        return part[p].at[chunk, pl.ds(2 * s, 2)]

    ring = {}

    def send_ring(p, direction, s, hop):
        sign = 1 if direction == 0 else -1
        chunk = (place[p] + sign * (4 - hop)) % RING
        if hop > (0 if s in far_end[direction] else 1):
            ring[p, direction, s, hop - 1].wait_recv()
            part[p][chunk, pl.ds(2 * s, 2)] += ring_in[p, direction, s, hop - 1]
        copy = remote(
            piece(p, chunk, s), ring_in.at[p, direction, s, hop],
            ring_send.at[p, direction, s, hop], ring_recv.at[p, direction, s, hop],
            first_axis[p](sign),
        )
        copy.start()
        ring[p, direction, s, hop] = copy

    def round_of(far, hop):
        for s in order:
            for p in range(2):
                for direction in range(2):
                    if (s in far_end[direction]) == far:
                        send_ring(p, direction, s, hop)

    def partial(b):
        local_a[b].wait()
        exchange[1 + b].wait_recv()
        product = lax.dot_general(
            a_all[:, pl.ds(b * 512, 512)], k_all[...], (((0,), (0,)), ((), ())),
            preferred_element_type=jnp.float32,
        )
        for p in range(2):
            tiles = [
                product[:, (2 * p + c) * 128 : (2 * p + c + 1) * 128].reshape(8, 8, 8, 128)
                for c in range(2)
            ]
            both = jnp.concatenate(tiles, axis=2).astype(jnp.bfloat16)
            for i in range(8):
                slot = (i - other[p] + 5) % RING
                part[p][:, slot, b] = both[i] if p == 0 else both[:, i]

    local_k.wait()
    exchange[0].wait_recv()
    for b in range(YLO):
        partial(b)
    round_of(True, 0)
    round_of(False, 1)

    grads = {}

    def input_grads(slot, away):
        out = lax.dot_general(
            k_all[...], w_all[slot], (((1,), (1,)), ((), ())), preferred_element_type=jnp.float32
        ).astype(jnp.bfloat16)
        ig_own[slot] = out[:TOK]
        ig_sib[slot] = out[TOK:]
        where = columns((ylo + away) % YLO, core)
        local = pltpu.make_async_copy(ig_own.at[slot], ig.at[:, where], ig_loc.at[slot])
        local.start()
        copy = remote(
            ig_sib.at[slot], ig.at[:, where], ig_send.at[slot], ig_recv.at[slot], sibling
        )
        copy.start()
        grads[slot] = (local, copy)

    input_grads(0, 0)
    round_of(True, 1)
    round_of(False, 2)
    relay_weight()
    round_of(True, 2)
    round_of(False, 3)
    round_of(True, 3)

    second = {}
    for s in order:
        for p in range(2):
            total = part[p][place[p], pl.ds(2 * s, 2)].astype(jnp.float32)
            for direction in range(2):
                ring[p, direction, s, 3].wait_recv()
                total = total + ring_in[p, direction, s, 3].astype(jnp.float32)
            part[p][place[p], pl.ds(2 * s, 2)] = total.astype(jnp.bfloat16)
            for slot in (2 * s, 2 * s + 1):
                step = (slot + 3) % RING
                if step == 0:
                    continue
                copy = remote(
                    part[p].at[place[p], slot], s2_in.at[p, step],
                    s2_send.at[p, step], s2_recv.at[p, step], second_axis[p](step),
                )
                copy.start()
                second[p, step] = copy

    for direction, away in ((0, -1), (1, 1)):
        weight[direction, 1].wait_recv()
        input_grads(1 + direction, away)

    quads = [[], []]
    for p in range(2):
        total = part[p][place[p], 5].astype(jnp.float32)
        for step in (4, 3, 5, 2, 6, 1, 7):
            second[p, step].wait_recv()
            total = total + s2_in[p, step].astype(jnp.float32)
        for c in range(2):
            for upper in range(2):
                first = 8 * c + 4 * upper
                quads[upper].append(total[:, first : first + 4])
    for upper in range(2):
        rows_of = jnp.concatenate(quads[upper], axis=1)
        s3_out[pl.ds(YLO * upper, YLO)] = rows_of.astype(jnp.bfloat16)
    third = {}
    for step in (4, 3, 5, 2, 6, 1, 7):
        copy = remote(
            s3_out.at[(y + step) % RING], s3_in.at[step], s3_send.at[step], s3_recv.at[step],
            on_y(step),
        )
        copy.start()
        third[step] = copy
    for direction in range(2):
        weight[direction, 2].wait_recv()
    input_grads(3, 2)
    total = s3_out[y].astype(jnp.float32)
    for step in (1, 7, 2, 6, 3, 5, 4):
        third[step].wait_recv()
        total = total + s3_in[step].astype(jnp.float32)
    total = total * (1.0 / TOKENS ** 0.5)
    for c in range(4):
        wg[:, c * 128 : (c + 1) * 128] = total[4 * c : 4 * c + 4]

    for local, copy in grads.values():
        local.wait()
        copy.wait()
    for copy in exchange:
        copy.wait_send()
    for group in (weight, ring, second, third):
        for copy in group.values():
            copy.wait_send()


def hand_on(ig_in, wg_in, ig, wg, ig_buf, wg_buf, in_sems, out_sems):
    pieces = [(wg_in, wg_buf, wg)]
    for i in range(8):
        piece = pl.ds(i * 16, 16)
        pieces.append((ig_in.at[piece], ig_buf.at[piece], ig.at[piece]))
    loads = [pltpu.make_async_copy(p[0], p[1], in_sems.at[i]) for i, p in enumerate(pieces)]
    stores = [pltpu.make_async_copy(p[1], p[2], out_sems.at[i]) for i, p in enumerate(pieces)]
    for load in loads:
        load.start()
    for load, store in zip(loads, stores):
        load.wait()
        store.start()
    for store in stores:
        store.wait()


def on_device(activations, key_grads, w_blocks, w_scales, w_outliers, outlier_rows):
    bf16, dma = jnp.bfloat16, pltpu.SemaphoreType.DMA
    hbm, vmem = pl.BlockSpec(memory_space=pl.ANY), pl.BlockSpec(memory_space=pltpu.VMEM)
    shapes = (
        jax.ShapeDtypeStruct((TOK, D), bf16),
        jax.ShapeDtypeStruct((4, KW), jnp.float32),
    )
    results = pl.pallas_call(
        kernel,
        out_shape=shapes,
        in_specs=[hbm] * 6,
        out_specs=(hbm, vmem),
        scratch_shapes=[
            pltpu.VMEM((1, 4), bf16),
            pltpu.VMEM((8, KW), bf16),
            pltpu.SMEM((2, 32), jnp.int32),
            pltpu.VMEM((2 * TOK, D // 2), bf16),
            pltpu.VMEM((2 * TOK, KW), bf16),
            pltpu.VMEM((512, KW), bf16),
            pltpu.VMEM((4, 512, KW), bf16),
            pltpu.VMEM((8, 8, YLO, 16, 128), bf16),
            pltpu.VMEM((8, 8, YLO, 16, 128), bf16),
            pltpu.VMEM((2, 2, 4, 4, 2, YLO, 16, 128), bf16),
            pltpu.VMEM((2, 8, YLO, 16, 128), bf16),
            pltpu.VMEM((8, 16, 128), bf16),
            pltpu.VMEM((8, 16, 128), bf16),
            pltpu.VMEM((4, TOK, 512), bf16),
            pltpu.VMEM((4, TOK, 512), bf16),
            dma((9,)), dma((5,)), dma((5,)), dma((2, 3)), dma((2, 3)),
            dma((2, 2, 4, 4)), dma((2, 2, 4, 4)),
            dma((2, 8)), dma((2, 8)), dma((8,)), dma((8,)), dma((4,)), dma((4,)), dma((4,)),
        ],
        compiler_params=pltpu.CompilerParams(
            collective_id=0, has_side_effects=True, vmem_limit_bytes=VMEM_BYTES
        ),
        cost_estimate=pl.CostEstimate(
            flops=4 * TOK * D * KW, bytes_accessed=4 * 1024 * 1024, transcendentals=0
        ),
    )(
        activations, key_grads, w_blocks, w_scales.reshape(1, -1), w_outliers, outlier_rows.T
    )
    return pl.pallas_call(
        hand_on,
        out_shape=shapes,
        in_specs=[hbm] * 2,
        out_specs=(hbm, hbm),
        scratch_shapes=[
            pltpu.VMEM((TOK, D), bf16), pltpu.VMEM((4, KW), jnp.float32), dma((9,)), dma((9,))
        ],
        compiler_params=pltpu.CompilerParams(vmem_limit_bytes=VMEM_BYTES),
    )(*results)


def solution(mesh):
    both = P(("node", "dp"), None)
    return jax.shard_map(
        on_device,
        mesh=mesh,
        in_specs=(both, both, P("node", None), P("node", None), P("node", None), P()),
        out_specs=(both, both),
        check_vma=False,
    )
```

```python
import jax
import jax.numpy as jnp
from jax import lax
from jax.experimental import pallas as pl
from jax.experimental.pallas import tpu as pltpu
from jax.sharding import PartitionSpec as P

D = 4096
KW = 512
BLOCK = 128
TOK = 128
TOKENS = 131072
RING = 8
YLO = 4
VMEM_BYTES = 56 * 1024 * 1024
MESH = pl.DeviceIdType.MESH


def kernel(
    act, key, wq, scales_in, wout_in, rows_in,
    ig, wg,
    scales, wout, rows, a_all, k_all, w_raw, w_all, part0, part1, ring_in, s2_in, s3_out, s3_in, ig_own, ig_sib,
    loc_sem, ex_send, ex_recv, w_send, w_recv, ring_send, ring_recv,
    s2_send, s2_recv, s3_send, s3_recv, ig_loc, ig_send, ig_recv, token,
):
    node, dp = lax.axis_index("node"), lax.axis_index("dp")
    core, ylo = node % 2, node // 2
    z, x, yhi = dp // 16, (dp // 2) % 8, dp % 2
    y = yhi * 4 + ylo
    part = (part0, part1)
    place = (x, z)
    other = (z, x)

    def at(px, py, pz, pc):
        return ((py % 4) * 2 + pc, pz * 16 + px * 2 + py // 4)

    def on_x(step):
        return at((x + step) % RING, y, z, core)

    def on_y(step):
        return at(x, (y + step) % RING, z, core)

    def on_z(step):
        return at(x, y, (z + step) % RING, core)

    sibling = at(x, y, z, 1 - core)
    first_axis = (on_x, on_z)
    second_axis = (on_z, on_x)

    def columns(block, whose):
        return pl.ds(pl.multiple_of((2 * block + whose) * 512, 512), 512)

    def remote(src, dst, send, recv, device):
        return pltpu.make_async_remote_copy(
            src_ref=src, dst_ref=dst, send_sem=send, recv_sem=recv,
            device_id=device, device_id_type=MESH,
        )

    barrier = pltpu.get_barrier_semaphore()
    for step in (1, -1):
        for along in (on_x, on_y, on_z):
            pl.semaphore_signal(barrier, inc=1, device_id=along(step), device_id_type=MESH)
    pl.semaphore_signal(barrier, inc=1, device_id=sibling, device_id_type=MESH)

    local_w = pltpu.make_async_copy(wq, w_raw, loc_sem.at[0])
    local_k = pltpu.make_async_copy(key, k_all.at[pl.ds(0, TOK)], loc_sem.at[1])
    local_a = [
        pltpu.make_async_copy(
            act.at[:, columns(b, core)],
            a_all.at[pl.ds(0, TOK), pl.ds(b * 512, 512)],
            loc_sem.at[2 + b],
        )
        for b in range(YLO)
    ]
    small = [
        pltpu.make_async_copy(src, dst, loc_sem.at[6 + i])
        for i, (src, dst) in enumerate(((scales_in, scales), (wout_in, wout), (rows_in, rows)))
    ]
    for copy in (*small, local_w, local_k, *local_a):
        copy.start()

    pl.semaphore_wait(barrier, 7)

    def send_token(direction, r):
        pl.semaphore_signal(
            token.at[direction, r], inc=1, device_id=on_y(1 - 2 * direction), device_id_type=MESH
        )

    def take_token(direction, r):
        pl.semaphore_wait(token.at[direction, r], 1)

    for direction in range(2):
        send_token(direction, 0)

    exchange = [remote(key, k_all.at[pl.ds(TOK, TOK)], ex_send.at[4], ex_recv.at[4], sibling)]
    for b in range(YLO):
        exchange.append(
            remote(
                act.at[:, columns(b, 1 - core)],
                a_all.at[pl.ds(TOK, TOK), pl.ds(b * 512, 512)],
                ex_send.at[b], ex_recv.at[b], sibling,
            )
        )
    for copy in exchange:
        copy.start()

    for copy in (*small, local_w):
        copy.wait()
    scale = scales[...].astype(jnp.float32)
    extra = wout[...].astype(jnp.float32)
    spot = lax.broadcasted_iota(jnp.int32, (BLOCK, KW), 0)
    for b in range(4):
        values = w_raw[pl.ds(b * BLOCK, BLOCK), :].astype(jnp.float32) * scale[:, b : b + 1]
        for j in range(2):
            row = rows[j, node * 4 + b]
            values = jnp.where(spot == row, extra[2 * b + j : 2 * b + j + 1, :], values)
        w_all[0, pl.ds(b * BLOCK, BLOCK), :] = values.astype(jnp.bfloat16)

    def half(slot, index):
        return w_all.at[slot, pl.ds(index * 256, 256)]

    weight = {}
    for direction, step in ((0, 1), (1, -1)):
        for order in range(2):
            index = order if direction == 0 else 1 - order
            copy = remote(
                half(0, index), half(1 + direction, index),
                w_send.at[direction, order], w_recv.at[direction, order], on_y(step),
            )
            copy.start()
            weight[direction, order] = copy

    def relay_weight():
        for direction, step in ((0, 1), (1, -1)):
            weight[direction, 0].wait_recv()
            copy = remote(
                half(1 + direction, direction), half(3, direction),
                w_send.at[direction, 2], w_recv.at[direction, 2], on_y(step),
            )
            copy.start()
            weight[direction, 2] = copy

    order = (0, 1, 3, 2)
    far_end = ((0, 3), (1, 2))

    def piece(p, chunk, s):
        return part[p].at[chunk, pl.ds(2 * s, 2)]

    ring = {}

    def send_ring(p, direction, s, hop):
        sign = 1 if direction == 0 else -1
        chunk = (place[p] + sign * (4 - hop)) % RING
        if hop > (0 if s in far_end[direction] else 1):
            ring[p, direction, s, hop - 1].wait_recv()
            part[p][chunk, pl.ds(2 * s, 2)] += ring_in[p, direction, s, hop - 1]
        copy = remote(
            piece(p, chunk, s), ring_in.at[p, direction, s, hop],
            ring_send.at[p, direction, s, hop], ring_recv.at[p, direction, s, hop],
            first_axis[p](sign),
        )
        copy.start()
        ring[p, direction, s, hop] = copy

    def round_of(far, hop):
        for s in order:
            for p in range(2):
                for direction in range(2):
                    if (s in far_end[direction]) == far:
                        send_ring(p, direction, s, hop)

    def partial(b):
        local_a[b].wait()
        exchange[1 + b].wait_recv()
        product = lax.dot_general(
            a_all[:, pl.ds(b * 512, 512)], k_all[...], (((0,), (0,)), ((), ())),
            preferred_element_type=jnp.float32,
        )
        for p in range(2):
            tiles = [
                product[:, (2 * p + c) * 128 : (2 * p + c + 1) * 128].reshape(8, 8, 8, 128)
                for c in range(2)
            ]
            both = jnp.concatenate(tiles, axis=2).astype(jnp.bfloat16)
            for i in range(8):
                slot = (i - other[p] + 5) % RING
                part[p][:, slot, b] = both[i] if p == 0 else both[:, i]

    local_k.wait()
    exchange[0].wait_recv()
    for b in range(YLO):
        partial(b)
    round_of(True, 0)
    round_of(False, 1)

    grads = {}

    def input_grads(slot, away):
        out = lax.dot_general(
            k_all[...], w_all[slot], (((1,), (1,)), ((), ())), preferred_element_type=jnp.float32
        ).astype(jnp.bfloat16)
        ig_own[slot] = out[:TOK]
        ig_sib[slot] = out[TOK:]
        where = columns((ylo + away) % YLO, core)
        local = pltpu.make_async_copy(ig_own.at[slot], ig.at[:, where], ig_loc.at[slot])
        local.start()
        copy = remote(
            ig_sib.at[slot], ig.at[:, where], ig_send.at[slot], ig_recv.at[slot], sibling
        )
        copy.start()
        grads[slot] = (local, copy)

    def drain(pair):
        for copy in pair:
            copy.wait()

    input_grads(0, 0)
    round_of(True, 1)
    for direction in range(2):
        take_token(direction, 0)
        send_token(direction, 1)
    round_of(False, 2)
    relay_weight()
    round_of(True, 2)
    for direction in range(2):
        take_token(direction, 1)
    send_token(0, 2)
    round_of(False, 3)
    round_of(True, 3)
    take_token(0, 2)

    second = {}
    for s in order:
        for p in range(2):
            total = part[p][place[p], pl.ds(2 * s, 2)].astype(jnp.float32)
            for direction in range(2):
                ring[p, direction, s, 3].wait_recv()
                total = total + ring_in[p, direction, s, 3].astype(jnp.float32)
            part[p][place[p], pl.ds(2 * s, 2)] = total.astype(jnp.bfloat16)
        for p in range(2):
            for slot in (2 * s, 2 * s + 1):
                step = (slot + 3) % RING
                if step == 0:
                    continue
                copy = remote(
                    part[p].at[place[p], slot], s2_in.at[p, step],
                    s2_send.at[p, step], s2_recv.at[p, step], second_axis[p](step),
                )
                copy.start()
                second[p, step] = copy

    for direction, away in ((0, -1), (1, 1)):
        weight[direction, 1].wait_recv()
        input_grads(1 + direction, away)

    for copy in (*exchange, *ring.values()):
        copy.wait_send()

    quads = [[], []]
    for p in range(2):
        total = part[p][place[p], 5].astype(jnp.float32)
        for step in (4, 3, 5, 2, 6, 1, 7):
            second[p, step].wait_recv()
            total = total + s2_in[p, step].astype(jnp.float32)
        for c in range(2):
            for upper in range(2):
                first = 8 * c + 4 * upper
                quads[upper].append(total[:, first : first + 4])
    for upper in range(2):
        rows_of = jnp.concatenate(quads[upper], axis=1)
        s3_out[pl.ds(YLO * upper, YLO)] = rows_of.astype(jnp.bfloat16)
    third = {}
    for step in (4, 3, 5, 2, 6, 1, 7):
        copy = remote(
            s3_out.at[(y + step) % RING], s3_in.at[step], s3_send.at[step], s3_recv.at[step],
            on_y(step),
        )
        copy.start()
        third[step] = copy
    for direction in range(2):
        weight[direction, 2].wait_recv()
    input_grads(3, 2)
    for copy in (*second.values(), *weight.values()):
        copy.wait_send()
    for slot in range(3):
        drain(grads.pop(slot))
    total = s3_out[y].astype(jnp.float32)
    for step in (1, 7, 2, 6, 3, 5, 4):
        third[step].wait_recv()
        total = total + s3_in[step].astype(jnp.float32)
    total = total * (1.0 / TOKENS ** 0.5)
    for c in range(4):
        wg[:, c * 128 : (c + 1) * 128] = total[4 * c : 4 * c + 4]

    for copy in third.values():
        copy.wait_send()
    drain(grads.pop(3))


def hand_on(ig_in, wg_in, ig, wg, sems):
    copies = [pltpu.make_async_copy(wg_in, wg, sems.at[8])]
    for i in range(8):
        piece = pl.ds(i * 16, 16)
        copies.append(pltpu.make_async_copy(ig_in.at[piece], ig.at[piece], sems.at[i]))
    for copy in copies:
        copy.start()
    for copy in copies:
        copy.wait()


def on_device(activations, key_grads, w_blocks, w_scales, w_outliers, outlier_rows):
    bf16, dma = jnp.bfloat16, pltpu.SemaphoreType.DMA
    hbm, vmem = pl.BlockSpec(memory_space=pl.ANY), pl.BlockSpec(memory_space=pltpu.VMEM)
    shapes = (
        jax.ShapeDtypeStruct((TOK, D), bf16),
        jax.ShapeDtypeStruct((4, KW), jnp.float32),
    )
    results = pl.pallas_call(
        kernel,
        out_shape=tuple(pltpu.VMEM(shape.shape, shape.dtype) for shape in shapes),
        in_specs=[hbm] * 6,
        out_specs=(hbm, vmem),
        scratch_shapes=[
            pltpu.VMEM((1, 4), bf16),
            pltpu.VMEM((8, KW), bf16),
            pltpu.SMEM((2, 32), jnp.int32),
            pltpu.VMEM((2 * TOK, D // 2), bf16),
            pltpu.VMEM((2 * TOK, KW), bf16),
            pltpu.VMEM((512, KW), bf16),
            pltpu.VMEM((4, 512, KW), bf16),
            pltpu.VMEM((8, 8, YLO, 16, 128), bf16),
            pltpu.VMEM((8, 8, YLO, 16, 128), bf16),
            pltpu.VMEM((2, 2, 4, 4, 2, YLO, 16, 128), bf16),
            pltpu.VMEM((2, 8, YLO, 16, 128), bf16),
            pltpu.VMEM((8, 16, 128), bf16),
            pltpu.VMEM((8, 16, 128), bf16),
            pltpu.VMEM((4, TOK, 512), bf16),
            pltpu.VMEM((4, TOK, 512), bf16),
            dma((9,)), dma((5,)), dma((5,)), dma((2, 3)), dma((2, 3)),
            dma((2, 2, 4, 4)), dma((2, 2, 4, 4)),
            dma((2, 8)), dma((2, 8)), dma((8,)), dma((8,)), dma((4,)), dma((4,)), dma((4,)),
            pltpu.SemaphoreType.REGULAR((2, 3)),
        ],
        compiler_params=pltpu.CompilerParams(
            collective_id=0, has_side_effects=True, vmem_limit_bytes=VMEM_BYTES
        ),
        cost_estimate=pl.CostEstimate(
            flops=4 * TOK * D * KW, bytes_accessed=4 * 1024 * 1024, transcendentals=0
        ),
    )(
        activations, key_grads, w_blocks, w_scales.reshape(1, -1), w_outliers, outlier_rows.T
    )
    return pl.pallas_call(
        hand_on,
        out_shape=shapes,
        in_specs=[vmem, vmem],
        out_specs=(hbm, hbm),
        scratch_shapes=[dma((9,))],
        compiler_params=pltpu.CompilerParams(vmem_limit_bytes=16 * 1024 * 1024),
    )(*results)


def solution(mesh):
    both = P(("node", "dp"), None)
    return jax.shard_map(
        on_device,
        mesh=mesh,
        in_specs=(both, both, P("node", None), P("node", None), P("node", None), P()),
        out_specs=(both, both),
        check_vma=False,
    )
```

```python
import jax
import jax.numpy as jnp
from jax import lax
from jax.experimental import pallas as pl
from jax.experimental.pallas import tpu as pltpu
from jax.sharding import PartitionSpec as P

D = 4096
KW = 512
BLOCK = 128
TOK = 128
TOKENS = 131072
RING = 8
YLO = 4
VMEM_BYTES = 56 * 1024 * 1024
MESH = pl.DeviceIdType.MESH


def kernel(
    act, key, wq, scales_in, wout_in, rows_in,
    ig, wg,
    scales, wout, rows, a_all, k_all, w_raw, w_all, part0, part1, ring_in, s2_in, s3_out, s3_in, ig_own, ig_sib,
    loc_sem, ex_send, ex_recv, w_send, w_recv, ring_send, ring_recv,
    s2_send, s2_recv, s3_send, s3_recv, ig_loc, ig_send, ig_recv, token,
):
    node, dp = lax.axis_index("node"), lax.axis_index("dp")
    core, ylo = node % 2, node // 2
    z, x, yhi = dp // 16, (dp // 2) % 8, dp % 2
    y = yhi * 4 + ylo
    part = (part0, part1)
    place = (x, z)
    other = (z, x)

    def at(px, py, pz, pc):
        return ((py % 4) * 2 + pc, pz * 16 + px * 2 + py // 4)

    def on_x(step):
        return at((x + step) % RING, y, z, core)

    def on_y(step):
        return at(x, (y + step) % RING, z, core)

    def on_z(step):
        return at(x, y, (z + step) % RING, core)

    sibling = at(x, y, z, 1 - core)
    first_axis = (on_x, on_z)
    second_axis = (on_z, on_x)

    def columns(block, whose):
        return pl.ds(pl.multiple_of((2 * block + whose) * 512, 512), 512)

    def remote(src, dst, send, recv, device):
        return pltpu.make_async_remote_copy(
            src_ref=src, dst_ref=dst, send_sem=send, recv_sem=recv,
            device_id=device, device_id_type=MESH,
        )

    barrier = pltpu.get_barrier_semaphore()
    for step in (1, -1):
        for along in (on_x, on_y, on_z):
            pl.semaphore_signal(barrier, inc=1, device_id=along(step), device_id_type=MESH)
    pl.semaphore_signal(barrier, inc=1, device_id=sibling, device_id_type=MESH)

    local_w = pltpu.make_async_copy(wq, w_raw, loc_sem.at[0])
    local_k = pltpu.make_async_copy(key, k_all.at[pl.ds(0, TOK)], loc_sem.at[1])
    local_a = [
        pltpu.make_async_copy(
            act.at[:, columns(b, core)],
            a_all.at[pl.ds(0, TOK), pl.ds(b * 512, 512)],
            loc_sem.at[2 + b],
        )
        for b in range(YLO)
    ]
    small = [
        pltpu.make_async_copy(src, dst, loc_sem.at[6 + i])
        for i, (src, dst) in enumerate(((scales_in, scales), (wout_in, wout), (rows_in, rows)))
    ]
    for copy in (*small, local_w, local_k, *local_a):
        copy.start()

    pl.semaphore_wait(barrier, 7)

    def send_token(direction, r):
        pl.semaphore_signal(
            token.at[direction, r], inc=1, device_id=on_y(1 - 2 * direction), device_id_type=MESH
        )

    def take_token(direction, r):
        pl.semaphore_wait(token.at[direction, r], 1)

    for direction in range(2):
        send_token(direction, 0)

    exchange = [remote(key, k_all.at[pl.ds(TOK, TOK)], ex_send.at[4], ex_recv.at[4], sibling)]
    for b in range(YLO):
        exchange.append(
            remote(
                act.at[:, columns(b, 1 - core)],
                a_all.at[pl.ds(TOK, TOK), pl.ds(b * 512, 512)],
                ex_send.at[b], ex_recv.at[b], sibling,
            )
        )
    for copy in exchange:
        copy.start()

    for copy in (*small, local_w):
        copy.wait()
    scale = scales[...].astype(jnp.float32)
    extra = wout[...].astype(jnp.float32)
    spot = lax.broadcasted_iota(jnp.int32, (BLOCK, KW), 0)
    for b in range(4):
        values = w_raw[pl.ds(b * BLOCK, BLOCK), :].astype(jnp.float32) * scale[:, b : b + 1]
        for j in range(2):
            row = rows[j, node * 4 + b]
            values = jnp.where(spot == row, extra[2 * b + j : 2 * b + j + 1, :], values)
        w_all[0, pl.ds(b * BLOCK, BLOCK), :] = values.astype(jnp.bfloat16)

    def half(slot, index):
        return w_all.at[slot, pl.ds(index * 256, 256)]

    weight = {}
    for direction, step in ((0, 1), (1, -1)):
        for order in range(2):
            index = order if direction == 0 else 1 - order
            copy = remote(
                half(0, index), half(1 + direction, index),
                w_send.at[direction, order], w_recv.at[direction, order], on_y(step),
            )
            copy.start()
            weight[direction, order] = copy

    def relay_weight():
        for direction, step in ((0, 1), (1, -1)):
            weight[direction, 0].wait_recv()
            copy = remote(
                half(1 + direction, direction), half(3, direction),
                w_send.at[direction, 2], w_recv.at[direction, 2], on_y(step),
            )
            copy.start()
            weight[direction, 2] = copy

    order = (0, 1, 3, 2)
    far_end = ((0, 3), (1, 2))

    def piece(p, chunk, s):
        return part[p].at[chunk, pl.ds(2 * s, 2)]

    ring = {}

    def send_ring(p, direction, s, hop):
        sign = 1 if direction == 0 else -1
        chunk = (place[p] + sign * (4 - hop)) % RING
        if hop > (0 if s in far_end[direction] else 1):
            ring[p, direction, s, hop - 1].wait_recv()
            part[p][chunk, pl.ds(2 * s, 2)] += ring_in[p, direction, s, hop - 1]
        copy = remote(
            piece(p, chunk, s), ring_in.at[p, direction, s, hop],
            ring_send.at[p, direction, s, hop], ring_recv.at[p, direction, s, hop],
            first_axis[p](sign),
        )
        copy.start()
        ring[p, direction, s, hop] = copy

    def round_of(far, hop):
        for s in order:
            for p in range(2):
                for direction in range(2):
                    if (s in far_end[direction]) == far:
                        send_ring(p, direction, s, hop)

    def partial(b):
        local_a[b].wait()
        exchange[1 + b].wait_recv()
        product = lax.dot_general(
            a_all[:, pl.ds(b * 512, 512)], k_all[...], (((0,), (0,)), ((), ())),
            preferred_element_type=jnp.float32,
        )
        for p in range(2):
            tiles = [
                product[:, (2 * p + c) * 128 : (2 * p + c + 1) * 128].reshape(8, 8, 8, 128)
                for c in range(2)
            ]
            both = jnp.concatenate(tiles, axis=2).astype(jnp.bfloat16)
            for i in range(8):
                slot = (i - other[p] + 5) % RING
                part[p][:, slot, b] = both[i] if p == 0 else both[:, i]

    local_k.wait()
    exchange[0].wait_recv()
    for b in range(YLO):
        partial(b)
    round_of(True, 0)
    round_of(False, 1)

    grads = {}

    def input_grads(slot, away):
        out = lax.dot_general(
            k_all[...], w_all[slot], (((1,), (1,)), ((), ())), preferred_element_type=jnp.float32
        ).astype(jnp.bfloat16)
        ig_own[slot] = out[:TOK]
        ig_sib[slot] = out[TOK:]
        where = columns((ylo + away) % YLO, core)
        local = pltpu.make_async_copy(ig_own.at[slot], ig.at[:, where], ig_loc.at[slot])
        local.start()
        copy = remote(
            ig_sib.at[slot], ig.at[:, where], ig_send.at[slot], ig_recv.at[slot], sibling
        )
        copy.start()
        grads[slot] = (local, copy)

    def drain(pair):
        for copy in pair:
            copy.wait()

    input_grads(0, 0)
    round_of(True, 1)
    for direction in range(2):
        take_token(direction, 0)
        send_token(direction, 1)
    round_of(False, 2)
    relay_weight()
    round_of(True, 2)
    for direction in range(2):
        take_token(direction, 1)
    send_token(0, 2)
    round_of(False, 3)
    round_of(True, 3)
    take_token(0, 2)

    second = {}

    def finish_ring(p, s):
        total = part[p][place[p], pl.ds(2 * s, 2)].astype(jnp.float32)
        for direction in range(2):
            ring[p, direction, s, 3].wait_recv()
            total = total + ring_in[p, direction, s, 3].astype(jnp.float32)
        part[p][place[p], pl.ds(2 * s, 2)] = total.astype(jnp.bfloat16)

    def send_second(p, s):
        for slot in (2 * s, 2 * s + 1):
            step = (slot + 3) % RING
            if step == 0:
                continue
            copy = remote(
                part[p].at[place[p], slot], s2_in.at[p, step],
                s2_send.at[p, step], s2_recv.at[p, step], second_axis[p](step),
            )
            copy.start()
            second[p, step] = copy

    for p in range(2):
        finish_ring(p, order[0])
    for p in range(2):
        send_second(p, order[0])
    for s in order[1:]:
        for p in range(2):
            finish_ring(p, s)
            send_second(p, s)

    for direction, away in ((0, -1), (1, 1)):
        weight[direction, 1].wait_recv()
        input_grads(1 + direction, away)

    for copy in (*exchange, *ring.values()):
        copy.wait_send()

    quads = [[], []]
    for p in range(2):
        total = part[p][place[p], 5].astype(jnp.float32)
        for step in (4, 3, 5, 2, 6, 1, 7):
            second[p, step].wait_recv()
            total = total + s2_in[p, step].astype(jnp.float32)
        for c in range(2):
            for upper in range(2):
                first = 8 * c + 4 * upper
                quads[upper].append(total[:, first : first + 4])
    for upper in range(2):
        rows_of = jnp.concatenate(quads[upper], axis=1)
        s3_out[pl.ds(YLO * upper, YLO)] = rows_of.astype(jnp.bfloat16)
    third = {}
    for step in (4, 3, 5, 2, 6, 1, 7):
        copy = remote(
            s3_out.at[(y + step) % RING], s3_in.at[step], s3_send.at[step], s3_recv.at[step],
            on_y(step),
        )
        copy.start()
        third[step] = copy
    for direction in range(2):
        weight[direction, 2].wait_recv()
    input_grads(3, 2)
    for copy in (*second.values(), *weight.values()):
        copy.wait_send()
    for slot in range(3):
        drain(grads.pop(slot))
    total = s3_out[y].astype(jnp.float32)
    for step in (1, 7, 2, 6, 3, 5, 4):
        third[step].wait_recv()
        total = total + s3_in[step].astype(jnp.float32)
    total = total * (1.0 / TOKENS ** 0.5)
    for c in range(4):
        wg[:, c * 128 : (c + 1) * 128] = total[4 * c : 4 * c + 4]

    for copy in third.values():
        copy.wait_send()
    drain(grads.pop(3))


def hand_on(ig_in, wg_in, ig, wg, sems):
    copies = [pltpu.make_async_copy(wg_in, wg, sems.at[8])]
    for i in range(8):
        piece = pl.ds(i * 16, 16)
        copies.append(pltpu.make_async_copy(ig_in.at[piece], ig.at[piece], sems.at[i]))
    for copy in copies:
        copy.start()
    for copy in copies:
        copy.wait()


def on_device(activations, key_grads, w_blocks, w_scales, w_outliers, outlier_rows):
    bf16, dma = jnp.bfloat16, pltpu.SemaphoreType.DMA
    hbm, vmem = pl.BlockSpec(memory_space=pl.ANY), pl.BlockSpec(memory_space=pltpu.VMEM)
    shapes = (
        jax.ShapeDtypeStruct((TOK, D), bf16),
        jax.ShapeDtypeStruct((4, KW), jnp.float32),
    )
    results = pl.pallas_call(
        kernel,
        out_shape=tuple(pltpu.VMEM(shape.shape, shape.dtype) for shape in shapes),
        in_specs=[hbm] * 6,
        out_specs=(hbm, vmem),
        scratch_shapes=[
            pltpu.VMEM((1, 4), bf16),
            pltpu.VMEM((8, KW), bf16),
            pltpu.SMEM((2, 32), jnp.int32),
            pltpu.VMEM((2 * TOK, D // 2), bf16),
            pltpu.VMEM((2 * TOK, KW), bf16),
            pltpu.VMEM((512, KW), bf16),
            pltpu.VMEM((4, 512, KW), bf16),
            pltpu.VMEM((8, 8, YLO, 16, 128), bf16),
            pltpu.VMEM((8, 8, YLO, 16, 128), bf16),
            pltpu.VMEM((2, 2, 4, 4, 2, YLO, 16, 128), bf16),
            pltpu.VMEM((2, 8, YLO, 16, 128), bf16),
            pltpu.VMEM((8, 16, 128), bf16),
            pltpu.VMEM((8, 16, 128), bf16),
            pltpu.VMEM((4, TOK, 512), bf16),
            pltpu.VMEM((4, TOK, 512), bf16),
            dma((9,)), dma((5,)), dma((5,)), dma((2, 3)), dma((2, 3)),
            dma((2, 2, 4, 4)), dma((2, 2, 4, 4)),
            dma((2, 8)), dma((2, 8)), dma((8,)), dma((8,)), dma((4,)), dma((4,)), dma((4,)),
            pltpu.SemaphoreType.REGULAR((2, 3)),
        ],
        compiler_params=pltpu.CompilerParams(
            collective_id=0, has_side_effects=True, vmem_limit_bytes=VMEM_BYTES
        ),
        cost_estimate=pl.CostEstimate(
            flops=4 * TOK * D * KW, bytes_accessed=4 * 1024 * 1024, transcendentals=0
        ),
    )(
        activations, key_grads, w_blocks, w_scales.reshape(1, -1), w_outliers, outlier_rows.T
    )
    return pl.pallas_call(
        hand_on,
        out_shape=shapes,
        in_specs=[vmem, vmem],
        out_specs=(hbm, hbm),
        scratch_shapes=[dma((9,))],
        compiler_params=pltpu.CompilerParams(vmem_limit_bytes=16 * 1024 * 1024),
    )(*results)


def solution(mesh):
    both = P(("node", "dp"), None)
    return jax.shard_map(
        on_device,
        mesh=mesh,
        in_specs=(both, both, P("node", None), P("node", None), P("node", None), P()),
        out_specs=(both, both),
        check_vma=False,
    )
```
